32 devices in a mesh: dp: 16 (over z, y, core), tensor: 2 (over x).
Axes of the slice: x: 2, y: 2, z: 4, core: 2. Of those that a mesh axis runs over, the one named last changes fastest.
Arguments:
- cand_ids: int32 [8192], P('dp'), may hold values from 0 to 128001, as said below
- val_ids: int32 [1024], P('dp'), may hold values from 0 to 128001, as said below
- inputs: bfloat16 [8192, 8192], P('dp', 'tensor'), may hold values from -6 to 6
- cotangent: bfloat16 [8192, 8192], P('dp'), may hold values from -6 to 6
- queries: bfloat16 [8192, 8192], P('dp', 'tensor'), may hold values from -16 to 16
- key_rows: bfloat16 [8192, 1024], P('dp', 'tensor'), may hold values from -16 to 16
- value_rows: bfloat16 [8192, 1024], P('dp', 'tensor'), may hold values from -6 to 6
- out_weight: bfloat16 [8192, 8192], P('tensor', 'dp'), may hold values from -0.0625 to 0.0625
- val_inputs: bfloat16 [1024, 8192], P('dp', 'tensor'), may hold values from -6 to 6
- val_cotangents: bfloat16 [1024, 8192], P('dp', 'tensor'), may hold values from -6 to 6
- val_attention: bfloat16 [1024, 8192], P('dp', 'tensor'), may hold values from -6 to 6
- val_query_grads: bfloat16 [1024, 8192], P('dp', 'tensor'), may hold values from -6 to 6
- val_keyvalue_grads: bfloat16 [1024, 2048], P('dp', 'tensor'), may hold values from -6 to 6
Outputs:
- scores: float32 [32, 4], P('dp')
The draws below stay inside these ranges and needn't reach their ends.
Inputs may be any that keep to these rules, and one draw needn't show every extreme that they name: `cand_ids`: each aligned run of 256 ids is one sequence: ids below 128001, then the padding id 128001 on at most 128 trailing positions. `val_ids`: each aligned run of 256 ids is one sequence: ids below 128001, then the padding id 128001 on at most 128 trailing positions.
All inputs are finite; a program needn't handle non-finite values.
Results may differ from the reference program's by a relative error of at most 0.02.
Values may be sent and summed in bfloat16 or wider, within the bound.
A program may use at most 256 MiB of HBM per device.

```python
import math
import jax
import jax.numpy as jnp
from jax import lax

D = 8192
HEADS = 64
KV = 8
HD = 128
LEN = 256
VALS = 4
TOKENS = 8192
VTOKENS = 1024
N_TENSOR = 2


pad_token = 128001


def token_draw(key, total):
    seq_count = total // LEN
    lengths = jax.random.randint(jax.random.fold_in(key, 1), (seq_count, 1), LEN // 2, LEN + 1)
    word_ids = jax.random.randint(jax.random.fold_in(key, 2), (seq_count, LEN), 0, pad_token)
    position = jnp.arange(LEN)[None, :]
    return jnp.where(position < lengths, word_ids, pad_token).reshape(total).astype(jnp.int32)


def draw_cand_ids(key, part):
    return token_draw(jax.random.fold_in(key, 3), TOKENS)


def draw_val_ids(key, part):
    return token_draw(jax.random.fold_in(key, 4), VTOKENS)


def base_noise(key, shape):
    return jnp.clip(jax.random.normal(key, shape, jnp.float32), -6.0, 6.0)


def draw_queries(key, part):
    noise = base_noise(jax.random.fold_in(key, 21), (TOKENS, HEADS * HD))
    return noise.astype(jnp.bfloat16)


def draw_key_rows(key, part):
    noise = base_noise(jax.random.fold_in(key, 22), (TOKENS, KV * HD))
    return noise.astype(jnp.bfloat16)


def block_levels(key, extent, split, low, high):
    factor_of, own = 1.0, jax.random.fold_in(key, 6)
    for dim, shards_of in split:
        draws = jnp.exp(jax.random.uniform(jax.random.fold_in(own, dim), (shards_of,), jnp.float32, low / len(split), high / len(split)))
        factor_of = factor_of * jnp.repeat(draws, extent[dim] // shards_of).reshape([-1 if axis == dim else 1 for axis in range(len(extent))])
    return factor_of


def bell_draw(own_key, shape, width, bound, cuts=(), kind=jnp.bfloat16):
    level = block_levels(own_key, shape, cuts, -0.22, 0.18) if cuts else 1.0
    result = jax.random.normal(own_key, shape, jnp.float32) * width * level
    return jnp.minimum(jnp.maximum(result, -bound), bound).astype(kind)


def setup_inputs(seed: int = 0) -> dict:
    streams_of = jax.random.split(jax.random.key(seed), 14)
    cand_ids = draw_cand_ids(jax.random.fold_in(streams_of[13], 71), 0)
    val_ids = draw_val_ids(jax.random.fold_in(streams_of[13], 71), 0)
    inputs = bell_draw(streams_of[2], (TOKENS, D), 1.0, 6.0, ((0, 16), (1, 2)))
    cotangent = bell_draw(streams_of[3], (TOKENS, D), 1.0, 6.0, ((0, 16),))
    queries = draw_queries(jax.random.fold_in(streams_of[13], 71), 0)
    key_rows = draw_key_rows(jax.random.fold_in(streams_of[13], 71), 0)
    value_rows = bell_draw(streams_of[6], (TOKENS, KV * HD), 1.0, 6.0, ((0, 16), (1, 2)))
    out_weight = bell_draw(streams_of[7], (HEADS * HD, D), (HEADS * HD) ** -0.5, 0.0625, ((0, 2), (1, 16)))
    val_inputs = bell_draw(streams_of[8], (VTOKENS, D), 1.0, 6.0, ((0, 16), (1, 2)))
    val_cotangents = bell_draw(streams_of[9], (VTOKENS, D), 1.0, 6.0, ((0, 16), (1, 2)))
    val_attention = bell_draw(streams_of[10], (VTOKENS, HEADS * HD), 1.0, 6.0, ((0, 16), (1, 2)))
    val_query_grads = bell_draw(streams_of[11], (VTOKENS, HEADS * HD), 1.0, 6.0, ((0, 16), (1, 2)))
    val_keyvalue_grads = bell_draw(streams_of[12], (VTOKENS, 2 * KV * HD), 1.0, 6.0, ((0, 16), (1, 2)))
    return {"cand_ids": cand_ids, "val_ids": val_ids, "inputs": inputs, "cotangent": cotangent, "queries": queries, "key_rows": key_rows, "value_rows": value_rows, "out_weight": out_weight, "val_inputs": val_inputs, "val_cotangents": val_cotangents, "val_attention": val_attention, "val_query_grads": val_query_grads, "val_keyvalue_grads": val_keyvalue_grads}


pad_token = 128001
rope_base = 500000.0

def rotation(seq_len, head_width):
    half_dim = head_width // 2
    inv_freq = rope_base ** (-(jnp.arange(half_dim).astype(jnp.float32) * 2.0 / head_width))
    angles = jnp.arange(seq_len).astype(jnp.float32)[:, None] * inv_freq[None, :]
    angles = jnp.concatenate([angles, angles], axis=1)
    return (jnp.cos(angles), jnp.sin(angles))

def turn_half(features):
    half_dim = features.shape[-1] // 2
    return jnp.concatenate([-features[..., half_dim:], features[..., :half_dim]], axis=-1)

def rounded(features):
    return lax.optimization_barrier(features.astype(jnp.bfloat16)).astype(jnp.float32)

def sequence_pass(pieces):
    query_raw, key_raw, value_part, grad_out = pieces
    seq_len, head_width = (key_raw.shape[0], key_raw.shape[-1])
    cos_table, sine_table = rotation(seq_len, head_width)
    score_scale = 1.0 / math.sqrt(head_width)
    q_float = query_raw.astype(jnp.float32)
    k_float = key_raw.astype(jnp.float32)
    query_rot = rounded(q_float * cos_table[:, None, None, :] + turn_half(q_float) * sine_table[:, None, None, :])
    key_rot = rounded(k_float * cos_table[:, None, :] + turn_half(k_float) * sine_table[:, None, :])
    value_float = value_part.astype(jnp.float32)
    grad_float = grad_out.astype(jnp.float32)
    logits = jnp.einsum('lkgd,mkd->kglm', query_rot, key_rot) * score_scale
    allowed = jnp.arange(seq_len)[None, :] <= jnp.arange(seq_len)[:, None]
    logits = jnp.where(allowed, logits, -jnp.inf)
    row_max = lax.optimization_barrier(jnp.max(logits, axis=-1, keepdims=True))
    raised = jnp.exp(logits - row_max)
    attn_probs = raised / lax.optimization_barrier(jnp.sum(raised, axis=-1, keepdims=True))
    probs_low = rounded(attn_probs)
    attended = jnp.einsum('kglm,mkd->lkgd', probs_low, value_float).astype(jnp.bfloat16)
    prob_grad = jnp.einsum('lkgd,mkd->kglm', grad_float, value_float)
    row_delta = lax.optimization_barrier(jnp.sum(attn_probs * prob_grad, axis=-1, keepdims=True))
    logit_grad = rounded(attn_probs * (prob_grad - row_delta) * score_scale)
    dquery = jnp.einsum('kglm,mkd->lkgd', logit_grad, key_rot)
    key_grad = jnp.einsum('kglm,lkgd->mkd', logit_grad, query_rot)
    dvalue = jnp.einsum('kglm,lkgd->mkd', probs_low, grad_float)
    dquery_raw = (dquery * cos_table[:, None, None, :] - turn_half(dquery) * sine_table[:, None, None, :]).astype(jnp.bfloat16)
    dkey_raw = (key_grad * cos_table[:, None, :] - turn_half(key_grad) * sine_table[:, None, :]).astype(jnp.bfloat16)
    return (attended, dquery_raw, jnp.stack([dkey_raw, dvalue.astype(jnp.bfloat16)], axis=2))

def block_gram(left, right):
    return jnp.dot(left, right.T, preferred_element_type=jnp.float32)

def reference(cand_ids, val_ids, inputs, cotangent, queries, key_rows, value_rows, out_weight, val_inputs, val_cotangents, val_attention, val_query_grads, val_keyvalue_grads):
    head_group = HEADS // KV
    seq_count = TOKENS // LEN
    live_rows = (cand_ids != pad_token).astype(jnp.float32)[:, None]
    masked = (cotangent.astype(jnp.float32) * live_rows).astype(jnp.bfloat16)
    grad_attn = jnp.dot(masked, out_weight.T, preferred_element_type=jnp.float32).astype(jnp.bfloat16)
    q_split = queries.reshape(seq_count, LEN, KV, head_group, HD)
    k_split = key_rows.reshape(seq_count, LEN, KV, HD)
    v_split = value_rows.reshape(seq_count, LEN, KV, HD)
    g_split = grad_attn.reshape(seq_count, LEN, KV, head_group, HD)
    attended, dquery, kv_grads = lax.map(sequence_pass, (q_split, k_split, v_split, g_split))
    attended = attended.reshape(TOKENS, HEADS * HD)
    dquery = dquery.reshape(TOKENS, HEADS * HD)
    kv_grads = kv_grads.reshape(TOKENS, 2 * KV * HD)
    val_live = (val_ids != pad_token).astype(jnp.float32)[:, None]
    val_dy = (val_cotangents.astype(jnp.float32) * val_live).astype(jnp.bfloat16)
    val_dq = (val_query_grads.astype(jnp.float32) * val_live).astype(jnp.bfloat16)
    val_dkv = (val_keyvalue_grads.astype(jnp.float32) * val_live).astype(jnp.bfloat16)
    d_block = D // N_TENSOR
    h_block = HEADS * HD // N_TENSOR
    k_block = 2 * KV * HD // N_TENSOR
    gram_attn = jnp.zeros((TOKENS, VTOKENS), jnp.float32)
    gram_cot = jnp.zeros((TOKENS, VTOKENS), jnp.float32)
    gram_input = jnp.zeros((TOKENS, VTOKENS), jnp.float32)
    gram_proj = jnp.zeros((TOKENS, VTOKENS), jnp.float32)
    for tensor_part in range(N_TENSOR):
        d_cut = slice(tensor_part * d_block, (tensor_part + 1) * d_block)
        h_cut = slice(tensor_part * h_block, (tensor_part + 1) * h_block)
        k_cut = slice(tensor_part * k_block, (tensor_part + 1) * k_block)
        gram_attn = gram_attn + rounded(block_gram(attended[:, h_cut], val_attention[:, h_cut]))
        gram_cot = gram_cot + rounded(block_gram(masked[:, d_cut], val_dy[:, d_cut]))
        gram_input = gram_input + rounded(block_gram(inputs[:, d_cut], val_inputs[:, d_cut]))
        gram_proj = gram_proj + rounded(block_gram(dquery[:, h_cut], val_dq[:, h_cut]) + block_gram(kv_grads[:, k_cut], val_dkv[:, k_cut]))
    product = gram_attn * gram_cot + gram_input * gram_proj
    return lax.optimization_barrier(jnp.sum(product.reshape(seq_count, LEN, VALS, LEN), axis=(1, 3))) * (1.0 / (64.0 * D))
```

```python
import math

import jax
import jax.numpy as jnp
from jax import lax
from jax.sharding import PartitionSpec as P

D = 8192
HEADS = 64
KV = 8
HD = 128
LEN = 256
VALS = 4


pad_token = 128001
rope_base = 500000.0


def rotation(seq_len, head_width):
    half_dim = head_width // 2
    inv_freq = rope_base ** (-(jnp.arange(half_dim).astype(jnp.float32) * 2.0 / head_width))
    angles = jnp.arange(seq_len).astype(jnp.float32)[:, None] * inv_freq[None, :]
    angles = jnp.concatenate([angles, angles], axis=1)
    return (jnp.cos(angles), jnp.sin(angles))


def turn_half(features):
    half_dim = features.shape[-1] // 2
    return jnp.concatenate([-features[..., half_dim:], features[..., :half_dim]], axis=-1)


def outer_rows(left, right):
    return lax.dot_general(
        left, right, (((1,), (1,)), ((), ())), preferred_element_type=jnp.float32
    )


def attend(query_raw, key_raw, value_part):
    seq_len, head_width = (key_raw.shape[1], key_raw.shape[-1])
    cos_table, sine_table = rotation(seq_len, head_width)
    score_scale = 1.0 / math.sqrt(head_width)
    q_cos = cos_table[None, :, None, None, :]
    q_sine = sine_table[None, :, None, None, :]
    k_cos = cos_table[None, :, None, :]
    k_sine = sine_table[None, :, None, :]
    q_float = query_raw.astype(jnp.float32)
    k_float = key_raw.astype(jnp.float32)
    query_rot = (q_float * q_cos + turn_half(q_float) * q_sine).astype(jnp.bfloat16)
    key_rot = (k_float * k_cos + turn_half(k_float) * k_sine).astype(jnp.bfloat16)
    logits = (
        jnp.einsum("slkgd,smkd->skglm", query_rot, key_rot, preferred_element_type=jnp.float32)
        * score_scale
    )
    allowed = jnp.arange(seq_len)[None, :] <= jnp.arange(seq_len)[:, None]
    logits = jnp.where(allowed, logits, -jnp.inf)
    row_max = jnp.max(logits, axis=-1, keepdims=True)
    raised = jnp.exp(logits - row_max)
    attn_probs = raised / jnp.sum(raised, axis=-1, keepdims=True)
    probs_low = attn_probs.astype(jnp.bfloat16)
    attended = jnp.einsum(
        "skglm,smkd->slkgd", probs_low, value_part, preferred_element_type=jnp.float32
    ).astype(jnp.bfloat16)
    return attended, (query_rot, key_rot, attn_probs, probs_low)


def attend_back(saved, value_part, grad_out):
    query_rot, key_rot, attn_probs, probs_low = saved
    seq_len, head_width = (key_rot.shape[1], key_rot.shape[-1])
    cos_table, sine_table = rotation(seq_len, head_width)
    score_scale = 1.0 / math.sqrt(head_width)
    q_cos = cos_table[None, :, None, None, :]
    q_sine = sine_table[None, :, None, None, :]
    k_cos = cos_table[None, :, None, :]
    k_sine = sine_table[None, :, None, :]
    prob_grad = jnp.einsum(
        "slkgd,smkd->skglm", grad_out, value_part, preferred_element_type=jnp.float32
    )
    row_delta = jnp.sum(attn_probs * prob_grad, axis=-1, keepdims=True)
    logit_grad = (attn_probs * (prob_grad - row_delta) * score_scale).astype(jnp.bfloat16)
    dquery = jnp.einsum(
        "skglm,smkd->slkgd", logit_grad, key_rot, preferred_element_type=jnp.float32
    )
    key_grad = jnp.einsum(
        "skglm,slkgd->smkd", logit_grad, query_rot, preferred_element_type=jnp.float32
    )
    dvalue = jnp.einsum(
        "skglm,slkgd->smkd", probs_low, grad_out, preferred_element_type=jnp.float32
    )
    dquery_raw = (dquery * q_cos - turn_half(dquery) * q_sine).astype(jnp.bfloat16)
    dkey_raw = (key_grad * k_cos - turn_half(key_grad) * k_sine).astype(jnp.bfloat16)
    return dquery_raw, jnp.stack([dkey_raw, dvalue.astype(jnp.bfloat16)], axis=3)


def exchange(parts, count):
    width = parts.shape[2] // count
    me = lax.axis_index("tensor")
    total = lax.dynamic_slice_in_dim(parts, me * width, width, 2).astype(jnp.float32)
    for step in range(1, count):
        target = lax.rem(me + step, count)
        sent = lax.dynamic_slice_in_dim(parts, target * width, width, 2)
        pairs = [(src, (src + step) % count) for src in range(count)]
        total = total + lax.ppermute(sent, "tensor", pairs).astype(jnp.float32)
    return total


def shards(
    cand_ids,
    val_ids,
    inputs,
    cotangent,
    queries,
    key_rows,
    value_rows,
    out_weight,
    val_inputs,
    val_cotangents,
    val_attention,
    val_query_grads,
    val_keyvalue_grads,
):
    tok_rows = cotangent.shape[0]
    seq_count = tok_rows // LEN
    kv_local = key_rows.shape[1] // HD
    head_group = HEADS // KV
    live_rows = (cand_ids != pad_token).astype(jnp.float32)[:, None]
    val_live = (val_ids != pad_token).astype(jnp.float32)[:, None]

    def val_masked(rows):
        return (rows.astype(jnp.float32) * val_live).astype(jnp.bfloat16)

    weight = lax.all_gather(out_weight, "dp", axis=1, tiled=True)
    early_rows = jnp.concatenate([val_attention, val_masked(val_cotangents), val_inputs], axis=1)
    late_rows = jnp.concatenate(
        [val_masked(val_query_grads), val_masked(val_keyvalue_grads)], axis=1
    )
    masked = (cotangent.astype(jnp.float32) * live_rows).astype(jnp.bfloat16)
    q_shape = (seq_count, LEN, kv_local, head_group, HD)
    kv_shape = (seq_count, LEN, kv_local, HD)
    value_part = value_rows.reshape(kv_shape)
    attended, saved = attend(queries.reshape(q_shape), key_rows.reshape(kv_shape), value_part)
    attended = attended.reshape(tok_rows, -1)
    weight, early_rows, late_rows, attended, masked = lax.optimization_barrier(
        (weight, early_rows, late_rows, attended, masked)
    )
    early = lax.all_gather(early_rows, "dp", axis=0, tiled=True)
    late = lax.all_gather(late_rows, "dp", axis=0, tiled=True)
    grad_attn = outer_rows(masked, weight).astype(jnp.bfloat16)
    dquery, kv_grads = attend_back(saved, value_part, grad_attn.reshape(q_shape))
    dquery = dquery.reshape(tok_rows, -1)
    kv_grads = kv_grads.reshape(tok_rows, -1)
    early, dquery, kv_grads = lax.optimization_barrier((early, dquery, kv_grads))
    feat_block = val_cotangents.shape[1]
    own_cotangent = lax.dynamic_slice_in_dim(
        masked, lax.axis_index("tensor") * feat_block, feat_block, 1
    )
    n_tensor = lax.axis_size("tensor")
    gram_attn = outer_rows(attended, early[:, :feat_block])
    gram_cot = outer_rows(own_cotangent, early[:, feat_block : 2 * feat_block])
    gram_input = outer_rows(inputs, early[:, 2 * feat_block :])
    early_share = exchange(
        jnp.stack([gram_attn, gram_cot, gram_input]).astype(jnp.bfloat16), n_tensor
    )
    gram_proj = outer_rows(dquery, late[:, :feat_block]) + outer_rows(
        kv_grads, late[:, feat_block:]
    )
    late_share = exchange(gram_proj[None].astype(jnp.bfloat16), n_tensor)
    factor = 1.0 / (64.0 * D)
    product = early_share[0] * early_share[1] + early_share[2] * late_share[0]
    col_width = product.shape[1]
    by_seq = jnp.sum(product.reshape(seq_count, LEN, col_width), axis=1)
    column = lax.axis_index("tensor") * col_width + jnp.arange(col_width)
    member = ((column // LEN)[:, None] == jnp.arange(VALS)[None, :]).astype(jnp.float32)
    partial_scores = jnp.sum(by_seq[:, :, None] * member[None, :, :], axis=1)
    return lax.psum(partial_scores, "tensor") * factor


def solution(mesh):
    return jax.shard_map(
        shards,
        mesh=mesh,
        in_specs=(
            P("dp"),
            P("dp"),
            P("dp", "tensor"),
            P("dp", None),
            P("dp", "tensor"),
            P("dp", "tensor"),
            P("dp", "tensor"),
            P("tensor", "dp"),
            P("dp", "tensor"),
            P("dp", "tensor"),
            P("dp", "tensor"),
            P("dp", "tensor"),
            P("dp", "tensor"),
        ),
        out_specs=P("dp", None),
        check_vma=False,
    )
```

```python
import functools
import math

import jax
import jax.numpy as jnp
from jax import lax
from jax.experimental import pallas as pl
from jax.experimental.pallas import tpu as pltpu
from jax.sharding import PartitionSpec as P

D = 8192
HEADS = 64
KV = 8
HD = 128
LEN = 256
VALS = 4


pad_token = 128001
rope_base = 500000.0


def rotation(seq_len, head_width):
    half_dim = head_width // 2
    inv_freq = rope_base ** (-(jnp.arange(half_dim).astype(jnp.float32) * 2.0 / head_width))
    angles = jnp.arange(seq_len).astype(jnp.float32)[:, None] * inv_freq[None, :]
    angles = jnp.concatenate([angles, angles], axis=1)
    return (jnp.cos(angles), jnp.sin(angles))


def outer_rows(left, right):
    return lax.dot_general(
        left, right, (((1,), (1,)), ((), ())), preferred_element_type=jnp.float32
    )


def attention_kernel(
    heads, query_ref, key_ref, value_ref, grad_ref, cos_ref, sine_ref, out_ref, dquery_ref, dkv_ref
):
    seq_len, head_width = key_ref.shape
    score_scale = 1.0 / math.sqrt(head_width)
    cos_table, sine_table = cos_ref[...], sine_ref[...]

    def turned(features):
        return pltpu.roll(features, head_width // 2, 1) * sine_table

    def product(left, right, left_dim, right_dim):
        return lax.dot_general(
            left, right, (((left_dim,), (right_dim,)), ((), ())), preferred_element_type=jnp.float32
        )

    key_float = key_ref[...].astype(jnp.float32)
    key_rot = (key_float * cos_table + turned(key_float)).astype(jnp.bfloat16)
    value_part = value_ref[...]
    allowed = lax.broadcasted_iota(jnp.int32, (seq_len, seq_len), 1) <= lax.broadcasted_iota(
        jnp.int32, (seq_len, seq_len), 0
    )
    key_grad = jnp.zeros((seq_len, head_width), jnp.float32)
    value_grad = jnp.zeros((seq_len, head_width), jnp.float32)
    for head in range(heads):
        columns = slice(head * head_width, (head + 1) * head_width)
        query_float = query_ref[:, columns].astype(jnp.float32)
        query_rot = (query_float * cos_table + turned(query_float)).astype(jnp.bfloat16)
        grad_out = grad_ref[:, columns]
        logits = product(query_rot, key_rot, 1, 1) * score_scale
        logits = jnp.where(allowed, logits, -jnp.inf)
        raised = jnp.exp(logits - jnp.max(logits, axis=1, keepdims=True))
        attn_probs = raised * (1.0 / jnp.sum(raised, axis=1, keepdims=True))
        probs_low = attn_probs.astype(jnp.bfloat16)
        out_ref[:, columns] = product(probs_low, value_part, 1, 0).astype(jnp.bfloat16)
        prob_grad = product(grad_out, value_part, 1, 1)
        row_delta = jnp.sum(attn_probs * prob_grad, axis=1, keepdims=True)
        logit_grad = (attn_probs * (prob_grad - row_delta) * score_scale).astype(jnp.bfloat16)
        dquery = product(logit_grad, key_rot, 1, 0)
        dquery_ref[:, columns] = (dquery * cos_table - turned(dquery)).astype(jnp.bfloat16)
        key_grad = key_grad + product(logit_grad, query_rot, 0, 0)
        value_grad = value_grad + product(probs_low, grad_out, 0, 0)
    dkv_ref[:, :head_width] = (key_grad * cos_table - turned(key_grad)).astype(jnp.bfloat16)
    dkv_ref[:, head_width:] = value_grad.astype(jnp.bfloat16)


def attention(queries, key_rows, value_rows, grad_attn):
    tok_rows, width = queries.shape
    kv_local = key_rows.shape[1] // HD
    heads = width // HD // kv_local
    cos_table, sine_table = rotation(LEN, HD)
    sign = jnp.where(jnp.arange(HD) < HD // 2, -1.0, 1.0)[None, :]
    wide = pl.BlockSpec((LEN, heads * HD), lambda seq, head: (seq, head))
    narrow = pl.BlockSpec((LEN, HD), lambda seq, head: (seq, head))
    table = pl.BlockSpec((LEN, HD), lambda seq, head: (0, 0))
    pairs = tok_rows * LEN * (width // HD)
    return pl.pallas_call(
        functools.partial(attention_kernel, heads),
        grid=(tok_rows // LEN, kv_local),
        in_specs=[wide, narrow, narrow, wide, table, table],
        out_specs=[wide, wide, pl.BlockSpec((LEN, 2 * HD), lambda seq, head: (seq, head))],
        out_shape=[
            jax.ShapeDtypeStruct((tok_rows, width), jnp.bfloat16),
            jax.ShapeDtypeStruct((tok_rows, width), jnp.bfloat16),
            jax.ShapeDtypeStruct((tok_rows, 2 * kv_local * HD), jnp.bfloat16),
        ],
        compiler_params=pltpu.CompilerParams(vmem_limit_bytes=32 * 1024 * 1024),
        cost_estimate=pl.CostEstimate(
            flops=12 * pairs * HD, bytes_accessed=10 * tok_rows * width, transcendentals=pairs
        ),
    )(queries, key_rows, value_rows, grad_attn, cos_table, sine_table * sign)


def unfold_kernel(joined_ref, late_ref):
    share, col_share = joined_ref.shape[0], late_ref.shape[1]
    for owner in range(late_ref.shape[0] // share):
        late_ref[owner * share : (owner + 1) * share, :] = joined_ref[
            :, owner * col_share : (owner + 1) * col_share
        ]


def unfold(joined, head_rows, share, width):
    n_dp = lax.axis_size("dp")
    col_share = joined.shape[1] // n_dp
    first = head_rows // share
    return pl.pallas_call(
        unfold_kernel,
        grid=(width // col_share,),
        in_specs=[pl.BlockSpec((share, joined.shape[1]), lambda block: (first + block, 0))],
        out_specs=pl.BlockSpec((n_dp * share, col_share), lambda block: (0, block)),
        out_shape=jax.ShapeDtypeStruct((n_dp * share, width), joined.dtype),
        compiler_params=pltpu.CompilerParams(vmem_limit_bytes=16 * 1024 * 1024),
        cost_estimate=pl.CostEstimate(
            flops=0, bytes_accessed=4 * n_dp * share * width, transcendentals=0
        ),
    )(joined)


def exchange(parts, count):
    width = parts.shape[1] // count
    me = lax.axis_index("tensor")
    total = lax.dynamic_slice_in_dim(parts, me * width, width, 1).astype(jnp.float32)
    for step in range(1, count):
        target = lax.rem(me + step, count)
        sent = lax.dynamic_slice_in_dim(parts, target * width, width, 1)
        pairs = [(src, (src + step) % count) for src in range(count)]
        total = total + lax.ppermute(sent, "tensor", pairs).astype(jnp.float32)
    return total


def shards(
    cand_ids,
    val_ids,
    inputs,
    cotangent,
    queries,
    key_rows,
    value_rows,
    out_weight,
    val_inputs,
    val_cotangents,
    val_attention,
    val_query_grads,
    val_keyvalue_grads,
):
    tok_rows = cotangent.shape[0]
    seq_count = tok_rows // LEN
    live_rows = (cand_ids != pad_token).astype(jnp.float32)[:, None]
    val_live = (val_ids != pad_token).astype(jnp.float32)[:, None]

    def val_masked(rows):
        return (rows.astype(jnp.float32) * val_live).astype(jnp.bfloat16)

    late_rows = jnp.concatenate(
        [val_masked(val_query_grads), val_masked(val_keyvalue_grads)], axis=1
    )
    head_rows, col_share = out_weight.shape
    val_share, late_width = late_rows.shape
    late_blocks = late_rows.reshape(val_share, late_width // col_share, col_share).swapaxes(0, 1)
    joined = lax.all_gather(
        jnp.concatenate([out_weight, late_blocks.reshape(-1, col_share)], axis=0),
        "dp", axis=1, tiled=True,
    )
    early_rows = jnp.concatenate([val_attention, val_masked(val_cotangents), val_inputs], axis=1)
    masked = (cotangent.astype(jnp.float32) * live_rows).astype(jnp.bfloat16)
    joined, early_rows, masked = lax.optimization_barrier((joined, early_rows, masked))
    early = lax.all_gather(early_rows, "dp", axis=0, tiled=True)
    grad_attn = outer_rows(masked, joined[:head_rows]).astype(jnp.bfloat16)
    attended, dquery, kv_grads = attention(queries, key_rows, value_rows, grad_attn)
    late = unfold(joined, head_rows, val_share, late_width)
    feat_block = val_cotangents.shape[1]
    own_cotangent = lax.dynamic_slice_in_dim(
        masked, lax.axis_index("tensor") * feat_block, feat_block, 1
    )
    n_tensor = lax.axis_size("tensor")
    gram_proj = outer_rows(dquery, late[:, :feat_block]) + outer_rows(
        kv_grads, late[:, feat_block:]
    )
    gram_proj = gram_proj.astype(jnp.bfloat16)
    early, gram_proj = lax.optimization_barrier((early, gram_proj))
    share_proj = exchange(gram_proj, n_tensor)
    grams = [
        exchange(outer_rows(left, early[:, at * feat_block : (at + 1) * feat_block]).astype(jnp.bfloat16), n_tensor)
        for at, left in enumerate((attended, own_cotangent, inputs))
    ]
    factor = 1.0 / (64.0 * D)
    product = grams[0] * grams[1] + grams[2] * share_proj
    col_width = product.shape[1]
    by_seq = jnp.sum(product.reshape(seq_count, LEN, col_width), axis=1)
    column = lax.axis_index("tensor") * col_width + jnp.arange(col_width)
    member = ((column // LEN)[:, None] == jnp.arange(VALS)[None, :]).astype(jnp.float32)
    partial_scores = jnp.sum(by_seq[:, :, None] * member[None, :, :], axis=1)
    return lax.psum(partial_scores, "tensor") * factor


def solution(mesh):
    return jax.shard_map(
        shards,
        mesh=mesh,
        in_specs=(
            P("dp"),
            P("dp"),
            P("dp", "tensor"),
            P("dp", None),
            P("dp", "tensor"),
            P("dp", "tensor"),
            P("dp", "tensor"),
            P("tensor", "dp"),
            P("dp", "tensor"),
            P("dp", "tensor"),
            P("dp", "tensor"),
            P("dp", "tensor"),
            P("dp", "tensor"),
        ),
        out_specs=P("dp", None),
        check_vma=False,
    )
```
